32 devices in a mesh: groups: 2 (over x), rows: 8 (over z, y), inner: 2 (over core).
Axes of the slice: x: 2, y: 2, z: 4, core: 2. Of those that a mesh axis runs over, the one named last changes fastest.
Arguments:
- embeddings: bfloat16 [131072, 1536], P(('groups', 'rows'), 'inner'), parts along dimension 0, may hold values from -7 to 7
- centroids: bfloat16 [16, 256, 1536], P(('groups', 'rows'), None, 'inner'), parts along dimension 0, may hold values from -9 to 9
- block_parent: int32 [256], P(('groups', 'rows')), parts along dimension 0, may hold values from 0 to 7, never falling along the last dimension, each value on 1 to 32 neighbouring positions
- block_size: int32 [256], P(('groups', 'rows')), parts along dimension 0, may hold values from 128 to 512
- owner_slot: int32 [16], P('groups'), parts along dimension 0, may hold values from 0 to 7, each once
Outputs:
- refined: bfloat16 [16, 256, 1536], P(('groups', 'rows'), None, 'inner'), parts along dimension 0
- child_mass: float32 [16, 256], P(('groups', 'rows')), parts along dimension 0
The draws below stay inside these ranges and needn't reach their ends.
There are 2 independent parts, one for each index of `groups`. The reference program is written for one: setup_inputs(seed, part) draws one part's arguments, and reference() takes and returns one part's arrays. A program takes and returns all parts, laid end to end along the dimension named above; each array names one. Nothing has to cross between parts.
Inputs may be any that keep to these rules, and one draw needn't show every extreme that they name: `block_parent`: never falling along the blocks; every parent has 1 to 32 blocks, one parent exactly that many. `owner_slot`: each parent's slot once.
All inputs are finite; a program needn't handle non-finite values.
Results may differ from the reference program's by a relative error of at most 0.008.
Values may be sent and summed in bfloat16 or wider, within the bound.
A program may use at most 128 MiB of HBM per device.

```python
import math
import jax
import jax.numpy as jnp
import numpy as np
from jax import lax

D = 1536
K = 256
BLK = 512
ROW_DEV = 8192
ITERS = 2
P_SIZE = 8
ROWS = 65536
NBLK = 128
N_ROWS = 8


def draw_embeddings(key, part):
    key = jax.random.fold_in(key, 11)
    first = jax.random.fold_in(key, 0)
    return jnp.clip(jax.random.normal(first, (ROWS, D), jnp.float32), -6.0, 6.0).astype(jnp.bfloat16)


def touch_ends(array, stream_key, smallest, top_value):
    shape = array.shape
    index_at = [jax.random.randint(jax.random.fold_in(stream_key, axis), (), 0, shape[axis]) for axis in range(len(shape))]
    array = array.at[tuple(index_at)].set(smallest)
    longest = shape.index(max(shape))
    index_at[longest] = (index_at[longest] + 1) % shape[longest]
    return array.at[tuple(index_at)].set(top_value)


def levels(stream_key, dims, pieces, low, high):
    gain, own = 1.0, jax.random.fold_in(stream_key, 6)
    for position, shards_of in pieces:
        draws = jnp.exp(jax.random.uniform(jax.random.fold_in(own, position), (shards_of,), jnp.float32, low / len(pieces), high / len(pieces)))
        gain = gain * jnp.repeat(draws, dims[position] // shards_of).reshape([-1 if axis == position else 1 for axis in range(len(dims))])
    return gain


def profile(number_of, total, bound, skew):
    portions = [(1 << 20) // math.isqrt(standing ** skew) + 1 for standing in range(2, number_of + 1)]
    surplus, counts = total - bound - (number_of - 1), [1] * (number_of - 1)
    while surplus > 0:
        free = [i for i in range(number_of - 1) if counts[i] < bound]
        whole, remaining = sum([portions[i] for i in free]), surplus
        for i in free:
            addition = min(bound - counts[i], max(1, remaining * portions[i] // whole), surplus)
            counts[i] = counts[i] + addition
            surplus = surplus - addition
    return np.array([bound] + counts)


def ragged_sizes(stream_key, amount, total, limit, skew):
    if amount == 2:
        one = jax.random.randint(stream_key, (), max(1, total - limit), min(limit, total - 1) + 1)
        return jnp.stack([one, total - one])
    lengths = jnp.asarray(profile(amount, total, limit, skew), jnp.int32)
    pairs = (amount - 1) // 2
    donor, receiver = lengths[1:1 + 2 * pairs:2], lengths[2:2 + 2 * pairs:2]
    margin = jnp.minimum(donor - 1, limit - receiver)
    shifted = jax.random.randint(jax.random.fold_in(stream_key, 1), (pairs,), 0, 1 << 20) % (margin + 1)
    lengths = lengths.at[1:1 + 2 * pairs:2].set(donor - shifted).at[2:2 + 2 * pairs:2].set(receiver + shifted)
    return lengths[jax.random.permutation(jax.random.fold_in(stream_key, 2), amount)]


def normal_values(key, shape, scale, limit, pieces=(), kind=jnp.bfloat16):
    array = scale * jax.random.normal(key, shape, jnp.float32)
    if pieces:
        array = array * levels(key, shape, pieces, -0.22, 0.18)
    return jnp.clip(array, -limit, limit).astype(kind)


def setup_inputs(seed: int = 0, part: int = 0) -> dict:
    key_list = jax.random.split(jax.random.key(seed), 6)
    own_keys = jax.random.split(jax.random.fold_in(key_list[5], part), 6)
    embeddings = draw_embeddings(jax.random.fold_in(jax.random.fold_in(key_list[5], part), 71), part)
    centroids = normal_values(own_keys[1], (P_SIZE, K, D), 1.5, 9.0, ((0, 8), (2, 2)))
    block_parent = jnp.searchsorted(jnp.cumsum(ragged_sizes(own_keys[2], P_SIZE, NBLK, NBLK // 4, 2)), jnp.arange(NBLK), side="right").astype(jnp.int32)
    block_size = touch_ends(jax.random.randint(own_keys[3], (NBLK,), BLK // 4, BLK + 1), jax.random.fold_in(own_keys[3], 1), BLK // 4, BLK).astype(jnp.int32)
    owner_slot = jax.random.permutation(own_keys[4], P_SIZE).astype(jnp.int32)
    return {"embeddings": embeddings, "centroids": centroids, "block_parent": block_parent, "block_size": block_size, "owner_slot": owner_slot}


def block_terms(points, center, size):
    row_square = lax.optimization_barrier(jnp.sum(jnp.square(points.astype(jnp.float32)), axis=1))
    center_square = lax.optimization_barrier(jnp.sum(jnp.square(center.astype(jnp.float32)), axis=1))
    cross_product = jnp.dot(points, center.T, preferred_element_type=jnp.float32)
    distance = row_square[:, None] + center_square[None, :] - 2.0 * cross_product
    valid = (jnp.arange(BLK, dtype=jnp.int32) < size).astype(jnp.float32)
    weight_rows = jax.nn.softmax(-distance * (0.5 / math.sqrt(D)), axis=1) * valid[:, None]
    sums = jnp.dot(weight_rows.astype(jnp.bfloat16).T, points, preferred_element_type=jnp.float32)
    return (sums, lax.optimization_barrier(jnp.sum(weight_rows, axis=0)))

def reference(embeddings, centroids, block_parent, block_size, owner_slot):
    per_device = ROW_DEV // BLK
    points = embeddings.reshape(N_ROWS, per_device, BLK, D)
    slots = owner_slot[block_parent].astype(jnp.int32).reshape(N_ROWS, per_device)
    sizes = block_size.reshape(N_ROWS, per_device)
    current = centroids
    total_mass = jnp.zeros((P_SIZE, K), jnp.float32)
    for sweep in range(ITERS):
        table = current

        def group(carry, inputs):
            group_points, group_slots, group_sizes = inputs

            def single(args):
                return block_terms(args[0], table[args[1]], args[2])
            sums, mass = lax.map(single, (group_points, group_slots, group_sizes))
            slot_sums = jnp.zeros((P_SIZE, K, D), jnp.float32).at[group_slots].add(sums)
            slot_mass = jnp.zeros((P_SIZE, K), jnp.float32).at[group_slots].add(mass)
            slot_sums = lax.optimization_barrier(slot_sums.astype(jnp.bfloat16)).astype(jnp.float32)
            slot_mass = lax.optimization_barrier(slot_mass.astype(jnp.bfloat16)).astype(jnp.float32)
            return ((carry[0] + slot_sums, carry[1] + slot_mass), None)
        start = (jnp.zeros((P_SIZE, K, D), jnp.float32), jnp.zeros((P_SIZE, K), jnp.float32))
        (total_sums, total_mass), _ = lax.scan(group, start, (points, slots, sizes))
        current = ((total_sums + current.astype(jnp.float32)) / (total_mass[:, :, None] + 1.0)).astype(jnp.bfloat16)
    return (current, total_mass)
```

```python
import functools
import math

import jax
import jax.numpy as jnp
from jax import lax
from jax.experimental import pallas as pl
from jax.experimental.pallas import tpu as pltpu
from jax.sharding import PartitionSpec as P

MESH = pl.DeviceIdType.MESH
BF = jnp.bfloat16
F32 = jnp.float32
EXTRA = 128
CHUNK = 32


def kernel(
    n, nslot, nb, reach, full_width,
    slot_ref, size_ref, last_ref, x_hbm, gathered_hbm, out_ref,
    x, table, own, sent, got, resp, acc, macc, seg, msg, near,
    x_sem, t_sem, d_send, d_recv, r_send, r_recv, n_send, n_recv,
):
    me = lax.axis_index("rows")
    core = lax.axis_index("inner")
    other = 1 - core
    rows = x.shape[0] // nb
    half = rows // 2
    kids, width = table.shape[1], table.shape[2]
    scale = 0.5 / math.sqrt(full_width) * math.log2(math.e)
    partner = {"inner": other}
    offsets = [-j for j in range(1, reach + 1)] + [j for j in range(1, reach + 1)]

    def x_copy(b):
        at = pl.ds(pl.multiple_of(b * rows, rows), rows)
        return pltpu.make_async_copy(x_hbm.at[at], x.at[at], x_sem.at[b])

    t_copy = pltpu.make_async_copy(gathered_hbm, table.at[pl.ds(0, nslot)], t_sem)
    t_copy.start()

    @pl.loop(0, nb)
    def _(b):
        x_copy(b).start()

    for i, off in enumerate(offsets):
        @pl.when(jnp.logical_or(me + off < 0, me + off >= n))
        def _():
            near[i] = jnp.full(near.shape[1:], -1.0, BF)

    barrier = pltpu.get_barrier_semaphore()
    pl.semaphore_signal(barrier, inc=1, device_id=partner, device_id_type=MESH)
    peers = 1
    for off in offsets:
        there = jnp.logical_and(me + off >= 0, me + off < n)
        peers = peers + jnp.where(there, 1, 0)

        @pl.when(there)
        def _():
            pl.semaphore_signal(
                barrier, inc=1, device_id={"rows": me + off}, device_id_type=MESH
            )
    pl.semaphore_wait(barrier, peers)

    def dist_copy(b):
        return pltpu.make_async_remote_copy(
            src_ref=sent.at[b], dst_ref=got.at[b], send_sem=d_send.at[b],
            recv_sem=d_recv.at[b], device_id=partner, device_id_type=MESH,
        )

    def resp_copy(b, part):
        return pltpu.make_async_remote_copy(
            src_ref=resp.at[b, part], dst_ref=resp.at[b, part], send_sem=r_send.at[b],
            recv_sem=r_recv.at[b], device_id=partner, device_id_type=MESH,
        )

    nt = (((1,), (1,)), ((), ()))

    def sweep(index_of, first):
        def dist_step(b):
            if first:
                x_copy(b).wait()
            c = table[index_of(b)]
            cf = c.astype(F32)
            square = jnp.sum(cf * cf, axis=1, keepdims=True)
            far = x[pl.ds(pl.multiple_of(b * rows + other * half, half), half), :]
            sent[b] = 2.0 * lax.dot_general(c, far, nt, preferred_element_type=F32) - square
            dist_copy(b).start()
            mine = x[pl.ds(pl.multiple_of(b * rows + core * half, half), half), :]
            own[b] = 2.0 * lax.dot_general(c, mine, nt, preferred_element_type=F32) - square

        def soft_step(b):
            dist_copy(b).wait()
            logit = (own[b] + got[b]) * scale
            e = jnp.exp2(logit - jnp.max(logit, axis=0, keepdims=True))
            place = lax.broadcasted_iota(jnp.int32, (1, half), 1) + core * half
            used = jnp.where(place < size_ref[b], 1.0, 0.0)
            r = e * (used / jnp.sum(e, axis=0, keepdims=True))
            resp[b, core] = r.astype(BF)
            resp_copy(b, core).start()

        def sum_step(b):
            resp_copy(b, core).wait_send()
            resp_copy(b, other).wait_recv()
            r0, r1 = resp[b, 0], resp[b, 1]
            lo = x[pl.ds(pl.multiple_of(b * rows, half), half), :]
            hi = x[pl.ds(pl.multiple_of(b * rows + half, half), half), :]
            mass = jnp.sum(r0.astype(F32) + r1.astype(F32), axis=1, keepdims=True)
            before = slot_ref[jnp.maximum(b - 1, 0)]
            keep = jnp.where(jnp.logical_and(b > 0, slot_ref[b] == before), 1.0, 0.0)
            total = (
                acc[...] * keep
                + jnp.dot(r0, lo, preferred_element_type=F32)
                + jnp.dot(r1, hi, preferred_element_type=F32)
            )
            acc[...] = total
            tally = macc[...] * keep + mass
            macc[...] = tally
            seg[b, :, :width] = total.astype(BF)
            lane = lax.broadcasted_iota(jnp.int32, (kids, EXTRA), 1)
            number = slot_ref[b].astype(F32)
            seg[b, :, width:] = jnp.where(lane < EXTRA // 2, tally, number).astype(BF)

        acc[...] = jnp.zeros_like(acc)
        macc[...] = jnp.zeros_like(macc)
        lag1, lag2 = 3, 6

        @pl.loop(0, nb + lag2)
        def _(step):
            @pl.when(step < nb)
            def _():
                dist_step(step)

            @pl.when(jnp.logical_and(step >= lag1, step < nb + lag1))
            def _():
                soft_step(step - lag1)

            @pl.when(step >= lag2)
            def _():
                sum_step(step - lag2)

    t_copy.wait()
    sweep(lambda b: slot_ref[b], True)

    head, tail = slot_ref[0], slot_ref[nb - 1]
    msg[0] = seg[last_ref[head]]
    msg[1] = seg[nb - 1]

    def near_copy(i, off):
        which = 0 if off < 0 else 1
        there = offsets.index(-off)
        return pltpu.make_async_remote_copy(
            src_ref=msg.at[which], dst_ref=near.at[there], send_sem=n_send.at[i],
            recv_sem=n_recv.at[there], device_id={"rows": me + off}, device_id_type=MESH,
        )

    def arrival(i):
        return pltpu.make_async_remote_copy(
            src_ref=msg.at[0], dst_ref=near.at[i], send_sem=n_send.at[i],
            recv_sem=n_recv.at[i], device_id={"rows": me}, device_id_type=MESH,
        )

    for i, off in enumerate(offsets):
        @pl.when(jnp.logical_and(me + off >= 0, me + off < n))
        def _():
            near_copy(i, off).start()

    table[nslot] = table[head]
    table[nslot + 1] = table[tail]

    def pieces(body):
        @pl.loop(0, kids // CHUNK)
        def _(c):
            body(pl.ds(pl.multiple_of(c * CHUNK, CHUNK), CHUNK))

    @pl.loop(0, nslot)
    def _(q):
        at = last_ref[q]

        def body(r):
            t = seg[at, r, :].astype(F32)
            new = (t[:, :width] + table[q, r, :].astype(F32)) / (t[:, width:width + 1] + 1.0)
            table[q, r, :] = new.astype(BF)

        pieces(body)

    for i, off in enumerate(offsets):
        @pl.when(jnp.logical_and(me + off >= 0, me + off < n))
        def _():
            near_copy(i, off).wait_send()
            arrival(i).wait_recv()

    ID = width + EXTRA // 2
    for which, number in ((0, head), (1, tail)):
        def body(r):
            t = msg[which, r, :].astype(F32)
            total = t[:, :width] + table[nslot + which, r, :].astype(F32)
            mass = t[:, width:width + 1] + 1.0
            for i in range(len(offsets)):
                m = near[i, r, :].astype(F32)
                flag = jnp.where(m[:, ID:ID + 1] == number.astype(F32), 1.0, 0.0)
                total = total + m[:, :width] * flag
                mass = mass + m[:, width:width + 1] * flag
            table[nslot + which, r, :] = (total / mass).astype(BF)

        pieces(body)

    def second(q):
        return jnp.where(q == head, nslot, jnp.where(q == tail, nslot + 1, q))

    sweep(lambda b: second(slot_ref[b]), False)

    @pl.loop(0, nslot)
    def _(q):
        at, where = last_ref[q], second(q)
        present = jnp.where(slot_ref[at] == q, 1.0, 0.0)
        is_head = jnp.where(q == head, 1.0, 0.0)

        def body(r):
            t = seg[at, r, :].astype(F32) * present
            ident = near[0, r, :].astype(F32)[:, ID:ID + 1]
            begun = jnp.where(ident == head.astype(F32), 1.0, 0.0) * is_head
            fold = present * (1.0 - begun)
            out_ref[q, r, :width] = (
                t[:, :width] + fold * table[where, r, :].astype(F32)
            ).astype(BF)
            out_ref[q, r, width:] = t[:, width:].astype(BF)

        pieces(body)


def on_device(embeddings, centroids, block_parent, block_size, owner_slot):
    nb = block_parent.shape[0]
    rows_all, width = embeddings.shape
    kids = centroids.shape[1]
    nslot = owner_slot.shape[0]
    n = lax.axis_size("rows")
    reach = -(-n // 4)
    half = rows_all // nb // 2
    slot_range = jnp.arange(nslot, dtype=jnp.int32)
    block_slot = jnp.sum(
        jnp.where(block_parent[:, None] == slot_range[None, :], owner_slot[None, :], 0), axis=1
    )
    place = jnp.arange(nb, dtype=jnp.int32)
    last = jnp.max(jnp.where(block_slot[:, None] == slot_range[None, :], place[:, None], 0), axis=0)
    gathered = lax.all_gather(centroids, "rows", axis=0, tiled=True)
    smem = pl.BlockSpec(memory_space=pltpu.SMEM)
    anywhere = pl.BlockSpec(memory_space=pl.ANY)
    dma = pltpu.SemaphoreType.DMA
    partial = pl.pallas_call(
        functools.partial(kernel, n, nslot, nb, reach, width * lax.axis_size("inner")),
        out_shape=jax.ShapeDtypeStruct((nslot, kids, width + EXTRA), BF),
        in_specs=[smem, smem, smem, anywhere, anywhere],
        out_specs=pl.BlockSpec(memory_space=pltpu.VMEM),
        scratch_shapes=[
            pltpu.VMEM((rows_all, width), BF),
            pltpu.VMEM((nslot + 2, kids, width), BF),
            pltpu.VMEM((nb, kids, half), F32),
            pltpu.VMEM((nb, kids, half), F32),
            pltpu.VMEM((nb, kids, half), F32),
            pltpu.VMEM((nb, 2, kids, half), BF),
            pltpu.VMEM((kids, width), F32),
            pltpu.VMEM((kids, EXTRA), F32),
            pltpu.VMEM((nb, kids, width + EXTRA), BF),
            pltpu.VMEM((2, kids, width + EXTRA), BF),
            pltpu.VMEM((2 * reach, kids, width + EXTRA), BF),
            dma((nb,)),
            dma,
            dma((nb,)),
            dma((nb,)),
            dma((nb,)),
            dma((nb,)),
            dma((2 * reach,)),
            dma((2 * reach,)),
        ],
        compiler_params=pltpu.CompilerParams(
            collective_id=0, has_side_effects=True, vmem_limit_bytes=60 * 1024 * 1024
        ),
        cost_estimate=pl.CostEstimate(
            flops=8 * rows_all * kids * width, bytes_accessed=embeddings.size * 2,
            transcendentals=2 * rows_all * kids // 2,
        ),
    )(block_slot, block_size, last, embeddings, gathered)
    total = lax.psum_scatter(partial, "rows", scatter_dimension=0, tiled=True).astype(F32)
    shard_mass = total[:, :, width]
    refined = (total[:, :, :width] / (shard_mass[:, :, None] + 1.0)).astype(BF)
    return (refined, shard_mass)


def solution(mesh):
    placed = (
        P(("groups", "rows"), "inner"),
        P(("groups", "rows"), None, "inner"),
        P(("groups", "rows")),
        P(("groups", "rows")),
        P("groups"),
    )
    return jax.shard_map(
        on_device,
        mesh=mesh,
        in_specs=placed,
        out_specs=(P(("groups", "rows"), None, "inner"), P(("groups", "rows"), None)),
        check_vma=False,
    )
```

```python
import functools
import math

import jax
import jax.numpy as jnp
from jax import lax
from jax.experimental import pallas as pl
from jax.experimental.pallas import tpu as pltpu
from jax.sharding import PartitionSpec as P

MESH = pl.DeviceIdType.MESH
BF = jnp.bfloat16
F32 = jnp.float32
EXTRA = 128
CHUNK = 32
PARTS = 4


def kernel(
    n, nslot, nb, reach, full_width,
    slot_ref, size_ref, last_ref, x_hbm, c_hbm, out_ref, mass_ref,
    x, table, own, sent, got, resp, acc, macc, seg, msg, near, ybuf, zbuf, mass_out, mass_in,
    x_sem, t_sem, d_send, d_recv, r_send, r_recv, n_send, n_recv,
    g_send, g_recv, y_send, y_recv, z_send, z_recv, m_send, m_recv,
):
    me = lax.axis_index("rows")
    core = lax.axis_index("inner")
    other = 1 - core
    rows = x.shape[0] // nb
    half = rows // 2
    kids, width = table.shape[1], table.shape[2]
    scale = 0.5 / math.sqrt(full_width) * math.log2(math.e)
    partner = {"inner": other}
    offsets = [-j for j in range(1, reach + 1)] + [j for j in range(1, reach + 1)]

    def x_copy(b):
        at = pl.ds(pl.multiple_of(b * rows, rows), rows)
        return pltpu.make_async_copy(x_hbm.at[at], x.at[at], x_sem.at[b])

    nz = n // 2
    z, y = me // 2, me % 2
    beside = me + 1 - 2 * y
    above, below = z < nz - 1, z > 0
    t_copy = pltpu.make_async_copy(c_hbm.at[0], table.at[me], t_sem)
    t_copy.start()

    @pl.loop(0, nb)
    def _(b):
        x_copy(b).start()

    for i, off in enumerate(offsets):
        @pl.when(jnp.logical_or(me + off < 0, me + off >= n))
        def _():
            near[i] = jnp.full(near.shape[1:], -1.0, BF)

    barrier = pltpu.get_barrier_semaphore()
    pl.semaphore_signal(barrier, inc=1, device_id=partner, device_id_type=MESH)
    for off in range(1, n):
        pl.semaphore_signal(
            barrier, inc=1, device_id={"rows": lax.rem(me + off, n)}, device_id_type=MESH
        )
    pl.semaphore_wait(barrier, n)

    def part(c):
        return pl.ds(pl.multiple_of(c * (kids // PARTS), kids // PARTS), kids // PARTS)

    def g_copy(way, s, c):
        to = (me + 2, me - 2, beside)[way]
        return pltpu.make_async_remote_copy(
            src_ref=table.at[s, part(c)], dst_ref=table.at[s, part(c)],
            send_sem=g_send.at[way, s, c], recv_sem=g_recv.at[s, c],
            device_id={"rows": to}, device_id_type=MESH,
        )

    def each_shard(do, arrive):
        @pl.loop(0, PARTS)
        def _(c):
            @pl.when(above)
            def _():
                do(g_copy(0, me, c))

            @pl.when(below)
            def _():
                do(g_copy(1, me, c))

            do(g_copy(2, me, c))

        for h in range(1, nz):
            @pl.loop(0, PARTS)
            def _(c):
                @pl.when(z >= h)
                def _():
                    s = me - 2 * h
                    arrive(s, c)

                    @pl.when(above)
                    def _():
                        do(g_copy(0, s, c))

                    do(g_copy(2, s, c))

                @pl.when(z + h < nz)
                def _():
                    s = me + 2 * h
                    arrive(s, c)

                    @pl.when(below)
                    def _():
                        do(g_copy(1, s, c))

                    do(g_copy(2, s, c))

    t_copy.wait()
    each_shard(lambda copy: copy.start(), lambda s, c: g_copy(2, s, c).wait_recv())
    for j in range(nz):
        @pl.loop(0, PARTS)
        def _(c):
            g_copy(2, 2 * j + 1 - y, c).wait_recv()

    def dist_copy(b):
        return pltpu.make_async_remote_copy(
            src_ref=sent.at[b], dst_ref=got.at[b], send_sem=d_send.at[b],
            recv_sem=d_recv.at[b], device_id=partner, device_id_type=MESH,
        )

    def resp_copy(b, part):
        return pltpu.make_async_remote_copy(
            src_ref=resp.at[b, part], dst_ref=resp.at[b, part], send_sem=r_send.at[b],
            recv_sem=r_recv.at[b], device_id=partner, device_id_type=MESH,
        )

    nt = (((1,), (1,)), ((), ()))

    def sweep(index_of, first):
        def dist_step(b):
            if first:
                x_copy(b).wait()
            c = table[index_of(b)]
            cf = c.astype(F32)
            square = jnp.sum(cf * cf, axis=1, keepdims=True)
            far = x[pl.ds(pl.multiple_of(b * rows + other * half, half), half), :]
            sent[b] = 2.0 * lax.dot_general(c, far, nt, preferred_element_type=F32) - square
            dist_copy(b).start()
            mine = x[pl.ds(pl.multiple_of(b * rows + core * half, half), half), :]
            own[b] = 2.0 * lax.dot_general(c, mine, nt, preferred_element_type=F32) - square

        def soft_step(b):
            dist_copy(b).wait()
            logit = (own[b] + got[b]) * scale
            e = jnp.exp2(logit - jnp.max(logit, axis=0, keepdims=True))
            place = lax.broadcasted_iota(jnp.int32, (1, half), 1) + core * half
            used = jnp.where(place < size_ref[b], 1.0, 0.0)
            r = e * (used / jnp.sum(e, axis=0, keepdims=True))
            resp[b, core] = r.astype(BF)
            resp_copy(b, core).start()

        def sum_step(b):
            resp_copy(b, core).wait_send()
            resp_copy(b, other).wait_recv()
            r0, r1 = resp[b, 0], resp[b, 1]
            lo = x[pl.ds(pl.multiple_of(b * rows, half), half), :]
            hi = x[pl.ds(pl.multiple_of(b * rows + half, half), half), :]
            mass = jnp.sum(r0.astype(F32) + r1.astype(F32), axis=1, keepdims=True)
            before = slot_ref[jnp.maximum(b - 1, 0)]
            keep = jnp.where(jnp.logical_and(b > 0, slot_ref[b] == before), 1.0, 0.0)
            total = (
                acc[...] * keep
                + jnp.dot(r0, lo, preferred_element_type=F32)
                + jnp.dot(r1, hi, preferred_element_type=F32)
            )
            acc[...] = total
            tally = macc[...] * keep + mass
            macc[...] = tally
            seg[b, :, :width] = total.astype(BF)
            lane = lax.broadcasted_iota(jnp.int32, (kids, EXTRA), 1)
            number = slot_ref[b].astype(F32)
            seg[b, :, width:] = jnp.where(lane < EXTRA // 2, tally, number).astype(BF)

        acc[...] = jnp.zeros_like(acc)
        macc[...] = jnp.zeros_like(macc)
        lag1, lag2 = 3, 6

        @pl.loop(0, nb + lag2)
        def _(step):
            @pl.when(step < nb)
            def _():
                dist_step(step)

            @pl.when(jnp.logical_and(step >= lag1, step < nb + lag1))
            def _():
                soft_step(step - lag1)

            @pl.when(step >= lag2)
            def _():
                sum_step(step - lag2)

    sweep(lambda b: slot_ref[b], True)

    head, tail = slot_ref[0], slot_ref[nb - 1]
    msg[0] = seg[last_ref[head]]
    msg[1] = seg[nb - 1]

    def near_copy(i, off):
        which = 0 if off < 0 else 1
        there = offsets.index(-off)
        return pltpu.make_async_remote_copy(
            src_ref=msg.at[which], dst_ref=near.at[there], send_sem=n_send.at[i],
            recv_sem=n_recv.at[there], device_id={"rows": me + off}, device_id_type=MESH,
        )

    def arrival(i):
        return pltpu.make_async_remote_copy(
            src_ref=msg.at[0], dst_ref=near.at[i], send_sem=n_send.at[i],
            recv_sem=n_recv.at[i], device_id={"rows": me}, device_id_type=MESH,
        )

    for i, off in enumerate(offsets):
        @pl.when(jnp.logical_and(me + off >= 0, me + off < n))
        def _():
            near_copy(i, off).start()

    each_shard(lambda copy: copy.wait_send(), lambda s, c: None)
    table[nslot] = table[head]
    table[nslot + 1] = table[tail]

    def pieces(body):
        @pl.loop(0, kids // CHUNK)
        def _(c):
            body(pl.ds(pl.multiple_of(c * CHUNK, CHUNK), CHUNK))

    @pl.loop(0, nslot)
    def _(q):
        at = last_ref[q]

        def body(r):
            t = seg[at, r, :].astype(F32)
            new = (t[:, :width] + table[q, r, :].astype(F32)) / (t[:, width:width + 1] + 1.0)
            table[q, r, :] = new.astype(BF)

        pieces(body)

    for i, off in enumerate(offsets):
        @pl.when(jnp.logical_and(me + off >= 0, me + off < n))
        def _():
            near_copy(i, off).wait_send()
            arrival(i).wait_recv()

    ID = width + EXTRA // 2
    for which, number in ((0, head), (1, tail)):
        def body(r):
            t = msg[which, r, :].astype(F32)
            total = t[:, :width] + table[nslot + which, r, :].astype(F32)
            mass = t[:, width:width + 1] + 1.0
            for i in range(len(offsets)):
                m = near[i, r, :].astype(F32)
                flag = jnp.where(m[:, ID:ID + 1] == number.astype(F32), 1.0, 0.0)
                total = total + m[:, :width] * flag
                mass = mass + m[:, width:width + 1] * flag
            table[nslot + which, r, :] = (total / mass).astype(BF)

        pieces(body)

    def second(q):
        return jnp.where(q == head, nslot, jnp.where(q == tail, nslot + 1, q))

    sweep(lambda b: second(slot_ref[b]), False)

    def mass_copy(to, source):
        return pltpu.make_async_remote_copy(
            src_ref=mass_out.at[to], dst_ref=mass_in.at[source], send_sem=m_send.at[to],
            recv_sem=m_recv.at[source], device_id={"rows": to}, device_id_type=MESH,
        )

    def make_partial(q):
        at, where = last_ref[q], second(q)
        present = jnp.where(slot_ref[at] == q, 1.0, 0.0)
        is_head = jnp.where(q == head, 1.0, 0.0)

        def body(r):
            t = seg[at, r, :width].astype(F32) * present
            ident = near[0, r, :].astype(F32)[:, ID:ID + 1]
            begun = jnp.where(ident == head.astype(F32), 1.0, 0.0) * is_head
            fold = present * (1.0 - begun)
            table[q, r, :] = (t + fold * table[where, r, :].astype(F32)).astype(BF)

        pieces(body)
        tile = jnp.transpose(seg[at, :, width:].astype(F32)) * present
        mass_out[q] = tile[:mass_out.shape[1], :].astype(BF)

    def y_copy(j, c):
        return pltpu.make_async_remote_copy(
            src_ref=table.at[2 * j + 1 - y, part(c)], dst_ref=ybuf.at[j, part(c)],
            send_sem=y_send.at[j, c], recv_sem=y_recv.at[j, c],
            device_id={"rows": beside}, device_id_type=MESH,
        )

    def z_copy(j, c, to, place):
        return pltpu.make_async_remote_copy(
            src_ref=table.at[2 * j + y, part(c)], dst_ref=zbuf.at[place, part(c)],
            send_sem=z_send.at[j, c], recv_sem=z_recv.at[place, c],
            device_id={"rows": to}, device_id_type=MESH,
        )

    def far_first(body):
        for t in range(nz - 1, 0, -1):
            @pl.when(z + t < nz)
            def _():
                body(t, 1)

            @pl.when(z >= t)
            def _():
                body(t, -1)

        body(0, 0)

    def send_beside(t, sign):
        j = z + sign * t
        make_partial(2 * j + 1 - y)

        @pl.loop(0, PARTS)
        def _(c):
            y_copy(j, c).start()

    far_first(send_beside)
    far_first(lambda t, sign: make_partial(2 * (z + sign * t) + y))
    for off in range(1, n):
        mass_copy(lax.rem(me + off, n), me).start()
    mass_in[me] = mass_out[me]

    def pass_on(t, sign):
        j = z + sign * t
        q = 2 * j + y

        @pl.loop(0, PARTS)
        def _(c):
            r = part(c)
            y_copy(j, c).wait_recv()
            if t > 0:
                table[q, r, :] = (table[q, r, :].astype(F32) + ybuf[j, r, :].astype(F32)).astype(BF)

                @pl.when(below if sign > 0 else above)
                def _():
                    z_copy(j, c, me, j).wait_recv()
                    table[q, r, :] = (
                        table[q, r, :].astype(F32) + zbuf[j, r, :].astype(F32)
                    ).astype(BF)

                if t == 1 and sign < 0:
                    z_copy(j, c, me - 2, nz).start()
                else:
                    z_copy(j, c, me + 2 * sign, j).start()
            else:
                acc[r, :] = table[me, r, :].astype(F32) + ybuf[z, r, :].astype(F32)

    far_first(pass_on)
    for off in range(1, n):
        mass_copy(me, lax.rem(me + off, n)).wait_recv()
    mass = mass_in[0].astype(F32)
    for s in range(1, n):
        mass = mass + mass_in[s].astype(F32)
    mass_ref[...] = mass[:1, :]
    column = jnp.transpose(jnp.broadcast_to(mass[:1, :], (EXTRA, kids)))
    macc[...] = column + 1.0

    @pl.loop(0, PARTS)
    def _(c):
        r = part(c)

        @pl.when(below)
        def _():
            z_copy(z, c, me, z).wait_recv()
            acc[r, :] = acc[r, :] + zbuf[z, r, :].astype(F32)

        @pl.when(above)
        def _():
            z_copy(z, c, me, nz).wait_recv()
            acc[r, :] = acc[r, :] + zbuf[nz, r, :].astype(F32)

        out_ref[0, r, :] = (acc[r, :] / macc[r, :1]).astype(BF)

    def sent_all(t, sign):
        j = z + sign * t

        @pl.loop(0, PARTS)
        def _(c):
            y_copy(j, c).wait_send()
            if t > 0:
                z_copy(j, c, me + 2 * sign, j).wait_send()

    far_first(sent_all)
    for off in range(1, n):
        mass_copy(lax.rem(me + off, n), me).wait_send()


def on_device(embeddings, centroids, block_parent, block_size, owner_slot):
    nb = block_parent.shape[0]
    rows_all, width = embeddings.shape
    kids = centroids.shape[1]
    nslot = owner_slot.shape[0]
    n = lax.axis_size("rows")
    reach = max(2, -(-n // 4))
    half = rows_all // nb // 2
    slot_range = jnp.arange(nslot, dtype=jnp.int32)
    block_slot = jnp.sum(
        jnp.where(block_parent[:, None] == slot_range[None, :], owner_slot[None, :], 0), axis=1
    )
    place = jnp.arange(nb, dtype=jnp.int32)
    last = jnp.max(jnp.where(block_slot[:, None] == slot_range[None, :], place[:, None], 0), axis=0)
    smem = pl.BlockSpec(memory_space=pltpu.SMEM)
    anywhere = pl.BlockSpec(memory_space=pl.ANY)
    dma = pltpu.SemaphoreType.DMA
    vmem = pl.BlockSpec(memory_space=pltpu.VMEM)
    return pl.pallas_call(
        functools.partial(kernel, n, nslot, nb, reach, width * lax.axis_size("inner")),
        out_shape=(
            jax.ShapeDtypeStruct((1, kids, width), BF),
            jax.ShapeDtypeStruct((1, kids), F32),
        ),
        in_specs=[smem, smem, smem, anywhere, anywhere],
        out_specs=(vmem, vmem),
        scratch_shapes=[
            pltpu.VMEM((rows_all, width), BF),
            pltpu.VMEM((nslot + 2, kids, width), BF),
            pltpu.VMEM((nb, kids, half), F32),
            pltpu.VMEM((nb, kids, half), F32),
            pltpu.VMEM((nb, kids, half), F32),
            pltpu.VMEM((nb, 2, kids, half), BF),
            pltpu.VMEM((kids, width), F32),
            pltpu.VMEM((kids, EXTRA), F32),
            pltpu.VMEM((nb, kids, width + EXTRA), BF),
            pltpu.VMEM((2, kids, width + EXTRA), BF),
            pltpu.VMEM((2 * reach, kids, width + EXTRA), BF),
            pltpu.VMEM((n // 2, kids, width), BF),
            pltpu.VMEM((n // 2 + 1, kids, width), BF),
            pltpu.VMEM((n, 16, kids), BF),
            pltpu.VMEM((n, 16, kids), BF),
            dma((nb,)),
            dma,
            dma((nb,)),
            dma((nb,)),
            dma((nb,)),
            dma((nb,)),
            dma((2 * reach,)),
            dma((2 * reach,)),
            dma((3, n, PARTS)),
            dma((n, PARTS)),
            dma((n // 2, PARTS)),
            dma((n // 2, PARTS)),
            dma((n // 2, PARTS)),
            dma((n // 2 + 1, PARTS)),
            dma((n,)),
            dma((n,)),
        ],
        compiler_params=pltpu.CompilerParams(
            collective_id=0, has_side_effects=True, vmem_limit_bytes=60 * 1024 * 1024
        ),
        cost_estimate=pl.CostEstimate(
            flops=8 * rows_all * kids * width, bytes_accessed=embeddings.size * 2,
            transcendentals=2 * rows_all * kids // 2,
        ),
    )(block_slot, block_size, last, embeddings, centroids)


def solution(mesh):
    placed = (
        P(("groups", "rows"), "inner"),
        P(("groups", "rows"), None, "inner"),
        P(("groups", "rows")),
        P(("groups", "rows")),
        P("groups"),
    )
    return jax.shard_map(
        on_device,
        mesh=mesh,
        in_specs=placed,
        out_specs=(P(("groups", "rows"), None, "inner"), P(("groups", "rows"), None)),
        check_vma=False,
    )
```

```python
import functools
import math

import jax
import jax.numpy as jnp
from jax import lax
from jax.experimental import pallas as pl
from jax.experimental.pallas import tpu as pltpu
from jax.sharding import PartitionSpec as P

MESH = pl.DeviceIdType.MESH
BF = jnp.bfloat16
F32 = jnp.float32
EXTRA = 128
CHUNK = 32
LAG1, LAG2 = 4, 8
PARTS = 4


def kernel(
    n, nslot, nb, reach, full_width,
    slot_ref, size_ref, last_ref, x_hbm, c_hbm, out_ref, mass_ref,
    x, table, own, sent, got, resp, acc, macc, seg, msg, near, ybuf, zbuf, mass_out, mass_in,
    x_sem, t_sem, d_send, d_recv, r_send, r_recv, n_send, n_recv,
    g_send, g_recv, y_send, y_recv, z_send, z_recv, m_send, m_recv,
):
    me = lax.axis_index("rows")
    core = lax.axis_index("inner")
    other = 1 - core
    rows = x.shape[0] // nb
    half = rows // 2
    kids, width = table.shape[1], table.shape[2]
    scale = 0.5 / math.sqrt(full_width) * math.log2(math.e)
    partner = {"inner": other}
    offsets = [-j for j in range(1, reach + 1)] + [j for j in range(1, reach + 1)]

    def x_copy(b):
        at = pl.ds(pl.multiple_of(b * rows, rows), rows)
        return pltpu.make_async_copy(x_hbm.at[at], x.at[at], x_sem.at[b])

    nz = n // 2
    z, y = me // 2, me % 2
    beside = me + 1 - 2 * y
    above, below = z < nz - 1, z > 0
    t_copy = pltpu.make_async_copy(c_hbm.at[0], table.at[me], t_sem)
    t_copy.start()

    @pl.loop(0, nb)
    def _(b):
        x_copy(b).start()

    for i, off in enumerate(offsets):
        @pl.when(jnp.logical_or(me + off < 0, me + off >= n))
        def _():
            near[i] = jnp.full(near.shape[1:], -1.0, BF)

    barrier = pltpu.get_barrier_semaphore()
    pl.semaphore_signal(barrier, inc=1, device_id=partner, device_id_type=MESH)
    for off in range(1, n):
        pl.semaphore_signal(
            barrier, inc=1, device_id={"rows": lax.rem(me + off, n)}, device_id_type=MESH
        )
    pl.semaphore_wait(barrier, n)

    def part(c):
        return pl.ds(pl.multiple_of(c * (kids // PARTS), kids // PARTS), kids // PARTS)

    def g_copy(way, s, c):
        to = (me + 2, me - 2, beside)[way]
        return pltpu.make_async_remote_copy(
            src_ref=table.at[s, part(c)], dst_ref=table.at[s, part(c)],
            send_sem=g_send.at[way, s, c], recv_sem=g_recv.at[s, c],
            device_id={"rows": to}, device_id_type=MESH,
        )

    def each_shard(do, arrive):
        @pl.loop(0, PARTS)
        def _(c):
            @pl.when(above)
            def _():
                do(g_copy(0, me, c))

            @pl.when(below)
            def _():
                do(g_copy(1, me, c))

            do(g_copy(2, me, c))

        for h in range(1, nz):
            @pl.loop(0, PARTS)
            def _(c):
                @pl.when(z >= h)
                def _():
                    s = me - 2 * h
                    arrive(s, c)

                    @pl.when(above)
                    def _():
                        do(g_copy(0, s, c))

                    do(g_copy(2, s, c))

                @pl.when(z + h < nz)
                def _():
                    s = me + 2 * h
                    arrive(s, c)

                    @pl.when(below)
                    def _():
                        do(g_copy(1, s, c))

                    do(g_copy(2, s, c))

    t_copy.wait()
    each_shard(lambda copy: copy.start(), lambda s, c: g_copy(2, s, c).wait_recv())
    for j in range(nz):
        @pl.loop(0, PARTS)
        def _(c):
            g_copy(2, 2 * j + 1 - y, c).wait_recv()

    def dist_copy(b):
        return pltpu.make_async_remote_copy(
            src_ref=sent.at[b], dst_ref=got.at[b], send_sem=d_send.at[b],
            recv_sem=d_recv.at[b], device_id=partner, device_id_type=MESH,
        )

    def resp_copy(b, part):
        return pltpu.make_async_remote_copy(
            src_ref=resp.at[b, part], dst_ref=resp.at[b, part], send_sem=r_send.at[b],
            recv_sem=r_recv.at[b], device_id=partner, device_id_type=MESH,
        )

    nt = (((1,), (1,)), ((), ()))

    def sweep(index_of, first):
        acc[...] = jnp.zeros_like(acc)
        macc[...] = jnp.zeros_like(macc)

        def body(dist, soft, summed):
            if dist is not None:
                if first:
                    x_copy(dist).wait()
                c = table[index_of(dist)]
                far = x[pl.ds(pl.multiple_of(dist * rows + other * half, half), half), :]
                mine = x[pl.ds(pl.multiple_of(dist * rows + core * half, half), half), :]
            if soft is not None:
                dist_copy(soft).wait()
                logit = (own[soft] + got[soft]) * scale
            if summed is not None:
                resp_copy(summed, core).wait_send()
                resp_copy(summed, other).wait_recv()
                r = jnp.concatenate([resp[summed, 0], resp[summed, 1]], axis=1)
                points = x[pl.ds(pl.multiple_of(summed * rows, rows), rows), :]
                before = slot_ref[jnp.maximum(summed - 1, 0)]
                keep = jnp.where(
                    jnp.logical_and(summed > 0, slot_ref[summed] == before), 1.0, 0.0
                )
            if dist is not None:
                cf = c.astype(F32)
                square = jnp.sum(cf * cf, axis=1, keepdims=True)
                away = 2.0 * lax.dot_general(c, far, nt, preferred_element_type=F32) - square
                sent[dist] = away
                here = 2.0 * lax.dot_general(c, mine, nt, preferred_element_type=F32) - square
                own[dist] = here
            if soft is not None:
                e = jnp.exp2(logit - jnp.max(logit, axis=0, keepdims=True))
                place = lax.broadcasted_iota(jnp.int32, (1, half), 1) + core * half
                used = jnp.where(place < size_ref[soft], 1.0, 0.0)
                resp[soft, core] = (e * (used / jnp.sum(e, axis=0, keepdims=True))).astype(BF)
            if summed is not None:
                total = acc[...] * keep + jnp.dot(r, points, preferred_element_type=F32)
                acc[...] = total
                seg[summed, :, :width] = total.astype(BF)
                tally = macc[...] * keep + jnp.sum(r.astype(F32), axis=1, keepdims=True)
                macc[...] = tally
                lane = lax.broadcasted_iota(jnp.int32, (kids, EXTRA), 1)
                number = slot_ref[summed].astype(F32)
                seg[summed, :, width:] = jnp.where(lane < EXTRA // 2, tally, number).astype(BF)
            if dist is not None:
                dist_copy(dist).start()
            if soft is not None:
                resp_copy(soft, core).start()

        marks = sorted({0, LAG1, LAG2, nb, nb + LAG1, nb + LAG2})
        for lo, hi in zip(marks[:-1], marks[1:]):
            @pl.loop(lo, hi)
            def _(step, lo=lo):
                body(
                    step if lo < nb else None,
                    step - LAG1 if LAG1 <= lo < nb + LAG1 else None,
                    step - LAG2 if LAG2 <= lo else None,
                )

    sweep(lambda b: slot_ref[b], True)

    head, tail = slot_ref[0], slot_ref[nb - 1]
    msg[0] = seg[last_ref[head]]
    msg[1] = seg[nb - 1]

    def near_copy(i, off, c):
        which = 0 if off < 0 else 1
        there = offsets.index(-off)
        return pltpu.make_async_remote_copy(
            src_ref=msg.at[which, part(c)], dst_ref=near.at[there, part(c)],
            send_sem=n_send.at[i, c], recv_sem=n_recv.at[there, c],
            device_id={"rows": me + off}, device_id_type=MESH,
        )

    def arrival(i, c):
        return pltpu.make_async_remote_copy(
            src_ref=msg.at[0, part(c)], dst_ref=near.at[i, part(c)], send_sem=n_send.at[i, c],
            recv_sem=n_recv.at[i, c], device_id={"rows": me}, device_id_type=MESH,
        )

    @pl.loop(0, PARTS)
    def _(c):
        for i, off in enumerate(offsets):
            @pl.when(jnp.logical_and(me + off >= 0, me + off < n))
            def _():
                near_copy(i, off, c).start()

    each_shard(lambda copy: copy.wait_send(), lambda s, c: None)
    table[nslot] = table[head]
    table[nslot + 1] = table[tail]

    def pieces(body):
        @pl.loop(0, kids // CHUNK)
        def _(c):
            body(pl.ds(pl.multiple_of(c * CHUNK, CHUNK), CHUNK))

    @pl.loop(0, nslot)
    def _(q):
        at = last_ref[q]

        def body(r):
            t = seg[at, r, :].astype(F32)
            new = (t[:, :width] + table[q, r, :].astype(F32)) / (t[:, width:width + 1] + 1.0)
            table[q, r, :] = new.astype(BF)

        pieces(body)

    ID = width + EXTRA // 2

    @pl.loop(0, PARTS)
    def _(c):
        for i, off in enumerate(offsets):
            @pl.when(jnp.logical_and(me + off >= 0, me + off < n))
            def _():
                near_copy(i, off, c).wait_send()
                arrival(i, c).wait_recv()

        for which, number in ((0, head), (1, tail)):
            @pl.loop(0, kids // PARTS // 16)
            def _(k):
                r = pl.ds(pl.multiple_of(c * (kids // PARTS) + k * 16, 16), 16)
                t = msg[which, r, :].astype(F32)
                total = t[:, :width] + table[nslot + which, r, :].astype(F32)
                mass = t[:, width:width + 1] + 1.0
                for i in range(len(offsets)):
                    m = near[i, r, :].astype(F32)
                    flag = jnp.where(m[:, ID:ID + 1] == number.astype(F32), 1.0, 0.0)
                    total = total + m[:, :width] * flag
                    mass = mass + m[:, width:width + 1] * flag
                table[nslot + which, r, :] = (total / mass).astype(BF)

    def second(q):
        return jnp.where(q == head, nslot, jnp.where(q == tail, nslot + 1, q))

    sweep(lambda b: second(slot_ref[b]), False)

    def mass_copy(to, source):
        return pltpu.make_async_remote_copy(
            src_ref=mass_out.at[to], dst_ref=mass_in.at[source], send_sem=m_send.at[to],
            recv_sem=m_recv.at[source], device_id={"rows": to}, device_id_type=MESH,
        )

    def make_partial(q):
        at, where = last_ref[q], second(q)
        present = jnp.where(slot_ref[at] == q, 1.0, 0.0)
        is_head = jnp.where(q == head, 1.0, 0.0)

        def body(r):
            t = seg[at, r, :width].astype(F32) * present
            ident = near[0, r, :].astype(F32)[:, ID:ID + 1]
            begun = jnp.where(ident == head.astype(F32), 1.0, 0.0) * is_head
            fold = present * (1.0 - begun)
            table[q, r, :] = (t + fold * table[where, r, :].astype(F32)).astype(BF)

        pieces(body)
        tile = jnp.transpose(seg[at, :, width:].astype(F32)) * present
        mass_out[q] = tile[:mass_out.shape[1], :].astype(BF)

    def y_copy(j, c):
        return pltpu.make_async_remote_copy(
            src_ref=table.at[2 * j + 1 - y, part(c)], dst_ref=ybuf.at[j, part(c)],
            send_sem=y_send.at[j, c], recv_sem=y_recv.at[j, c],
            device_id={"rows": beside}, device_id_type=MESH,
        )

    def z_copy(j, c, to, place):
        return pltpu.make_async_remote_copy(
            src_ref=table.at[2 * j + y, part(c)], dst_ref=zbuf.at[place, part(c)],
            send_sem=z_send.at[j, c], recv_sem=z_recv.at[place, c],
            device_id={"rows": to}, device_id_type=MESH,
        )

    def far_first(body):
        for t in range(nz - 1, 0, -1):
            @pl.when(z + t < nz)
            def _():
                body(t, 1)

            @pl.when(z >= t)
            def _():
                body(t, -1)

        body(0, 0)

    def send_beside(t, sign):
        j = z + sign * t
        make_partial(2 * j + 1 - y)

        @pl.loop(0, PARTS)
        def _(c):
            y_copy(j, c).start()

    far_first(send_beside)
    far_first(lambda t, sign: make_partial(2 * (z + sign * t) + y))
    for off in range(1, n):
        mass_copy(lax.rem(me + off, n), me).start()
    mass_in[me] = mass_out[me]

    def pass_on(t, sign):
        j = z + sign * t
        q = 2 * j + y

        @pl.loop(0, PARTS)
        def _(c):
            r = part(c)
            y_copy(j, c).wait_recv()
            if t > 0:
                table[q, r, :] = (table[q, r, :].astype(F32) + ybuf[j, r, :].astype(F32)).astype(BF)

                @pl.when(below if sign > 0 else above)
                def _():
                    z_copy(j, c, me, j).wait_recv()
                    table[q, r, :] = (
                        table[q, r, :].astype(F32) + zbuf[j, r, :].astype(F32)
                    ).astype(BF)

                if t == 1 and sign < 0:
                    z_copy(j, c, me - 2, nz).start()
                else:
                    z_copy(j, c, me + 2 * sign, j).start()
            else:
                acc[r, :] = table[me, r, :].astype(F32) + ybuf[z, r, :].astype(F32)

    far_first(pass_on)
    for off in range(1, n):
        mass_copy(me, lax.rem(me + off, n)).wait_recv()
    mass = mass_in[0].astype(F32)
    for s in range(1, n):
        mass = mass + mass_in[s].astype(F32)
    mass_ref[...] = mass[:1, :]
    column = jnp.transpose(jnp.broadcast_to(mass[:1, :], (EXTRA, kids)))
    macc[...] = column + 1.0

    @pl.loop(0, PARTS)
    def _(c):
        r = part(c)

        @pl.when(below)
        def _():
            z_copy(z, c, me, z).wait_recv()
            acc[r, :] = acc[r, :] + zbuf[z, r, :].astype(F32)

        @pl.when(above)
        def _():
            z_copy(z, c, me, nz).wait_recv()
            acc[r, :] = acc[r, :] + zbuf[nz, r, :].astype(F32)

        out_ref[0, r, :] = (acc[r, :] / macc[r, :1]).astype(BF)

    def sent_all(t, sign):
        j = z + sign * t

        @pl.loop(0, PARTS)
        def _(c):
            y_copy(j, c).wait_send()
            if t > 0:
                z_copy(j, c, me + 2 * sign, j).wait_send()

    far_first(sent_all)
    for off in range(1, n):
        mass_copy(lax.rem(me + off, n), me).wait_send()


def on_device(embeddings, centroids, block_parent, block_size, owner_slot):
    nb = block_parent.shape[0]
    rows_all, width = embeddings.shape
    kids = centroids.shape[1]
    nslot = owner_slot.shape[0]
    n = lax.axis_size("rows")
    reach = max(2, -(-n // 4))
    half = rows_all // nb // 2
    slot_range = jnp.arange(nslot, dtype=jnp.int32)
    block_slot = jnp.sum(
        jnp.where(block_parent[:, None] == slot_range[None, :], owner_slot[None, :], 0), axis=1
    )
    place = jnp.arange(nb, dtype=jnp.int32)
    last = jnp.max(jnp.where(block_slot[:, None] == slot_range[None, :], place[:, None], 0), axis=0)
    smem = pl.BlockSpec(memory_space=pltpu.SMEM)
    anywhere = pl.BlockSpec(memory_space=pl.ANY)
    dma = pltpu.SemaphoreType.DMA
    vmem = pl.BlockSpec(memory_space=pltpu.VMEM)
    return pl.pallas_call(
        functools.partial(kernel, n, nslot, nb, reach, width * lax.axis_size("inner")),
        out_shape=(
            jax.ShapeDtypeStruct((1, kids, width), BF),
            jax.ShapeDtypeStruct((1, kids), F32),
        ),
        in_specs=[smem, smem, smem, anywhere, anywhere],
        out_specs=(vmem, vmem),
        scratch_shapes=[
            pltpu.VMEM((rows_all, width), BF),
            pltpu.VMEM((nslot + 2, kids, width), BF),
            pltpu.VMEM((nb, kids, half), F32),
            pltpu.VMEM((nb, kids, half), F32),
            pltpu.VMEM((nb, kids, half), F32),
            pltpu.VMEM((nb, 2, kids, half), BF),
            pltpu.VMEM((kids, width), F32),
            pltpu.VMEM((kids, EXTRA), F32),
            pltpu.VMEM((nb, kids, width + EXTRA), BF),
            pltpu.VMEM((2, kids, width + EXTRA), BF),
            pltpu.VMEM((2 * reach, kids, width + EXTRA), BF),
            pltpu.VMEM((n // 2, kids, width), BF),
            pltpu.VMEM((n // 2 + 1, kids, width), BF),
            pltpu.VMEM((n, 16, kids), BF),
            pltpu.VMEM((n, 16, kids), BF),
            dma((nb,)),
            dma,
            dma((nb,)),
            dma((nb,)),
            dma((nb,)),
            dma((nb,)),
            dma((2 * reach, PARTS)),
            dma((2 * reach, PARTS)),
            dma((3, n, PARTS)),
            dma((n, PARTS)),
            dma((n // 2, PARTS)),
            dma((n // 2, PARTS)),
            dma((n // 2, PARTS)),
            dma((n // 2 + 1, PARTS)),
            dma((n,)),
            dma((n,)),
        ],
        compiler_params=pltpu.CompilerParams(
            collective_id=0, has_side_effects=True, vmem_limit_bytes=60 * 1024 * 1024
        ),
        cost_estimate=pl.CostEstimate(
            flops=8 * rows_all * kids * width, bytes_accessed=embeddings.size * 2,
            transcendentals=2 * rows_all * kids // 2,
        ),
    )(block_slot, block_size, last, embeddings, centroids)


def solution(mesh):
    placed = (
        P(("groups", "rows"), "inner"),
        P(("groups", "rows"), None, "inner"),
        P(("groups", "rows")),
        P(("groups", "rows")),
        P("groups"),
    )
    return jax.shard_map(
        on_device,
        mesh=mesh,
        in_specs=placed,
        out_specs=(P(("groups", "rows"), None, "inner"), P(("groups", "rows"), None)),
        check_vma=False,
    )
```

```python
import functools
import math

import jax
import jax.numpy as jnp
from jax import lax
from jax.experimental import pallas as pl
from jax.experimental.pallas import tpu as pltpu
from jax.sharding import PartitionSpec as P

MESH = pl.DeviceIdType.MESH
BF = jnp.bfloat16
F32 = jnp.float32
EXTRA = 128
CHUNK = 32
LAG1, LAG2 = 5, 10
PARTS = 4


def kernel(
    n, nslot, nb, reach, full_width,
    slot_ref, size_ref, last_ref, x_hbm, c_hbm, out_ref, mass_ref,
    x, table, own, sent, got, resp, acc, macc, seg, msg, near, ybuf, zbuf, mass_out, mass_in,
    x_sem, t_sem, d_send, d_recv, r_send, r_recv, n_send, n_recv,
    g_send, g_recv, y_send, y_recv, z_send, z_recv, m_send, m_recv,
):
    me = lax.axis_index("rows")
    core = lax.axis_index("inner")
    other = 1 - core
    rows = x.shape[0] // nb
    half = rows // 2
    kids, width = table.shape[1], table.shape[2]
    scale = 0.5 / math.sqrt(full_width) * math.log2(math.e)
    partner = {"inner": other}
    offsets = [-j for j in range(1, reach + 1)] + [j for j in range(1, reach + 1)]

    def x_copy(b):
        at = pl.ds(pl.multiple_of(b * rows, rows), rows)
        return pltpu.make_async_copy(x_hbm.at[at], x.at[at], x_sem.at[b])

    nz = n // 2
    z, y = me // 2, me % 2
    beside = me + 1 - 2 * y
    above, below = z < nz - 1, z > 0
    t_copy = pltpu.make_async_copy(c_hbm.at[0], table.at[me], t_sem)
    t_copy.start()

    @pl.loop(0, nb)
    def _(b):
        x_copy(b).start()

    for i, off in enumerate(offsets):
        @pl.when(jnp.logical_or(me + off < 0, me + off >= n))
        def _():
            near[i] = jnp.full(near.shape[1:], -1.0, BF)

    barrier = pltpu.get_barrier_semaphore()
    pl.semaphore_signal(barrier, inc=1, device_id=partner, device_id_type=MESH)
    for off in range(1, n):
        pl.semaphore_signal(
            barrier, inc=1, device_id={"rows": lax.rem(me + off, n)}, device_id_type=MESH
        )
    pl.semaphore_wait(barrier, n)

    def part(c):
        return pl.ds(pl.multiple_of(c * (kids // PARTS), kids // PARTS), kids // PARTS)

    def g_copy(way, s, c):
        to = (me + 2, me - 2, beside)[way]
        return pltpu.make_async_remote_copy(
            src_ref=table.at[s, part(c)], dst_ref=table.at[s, part(c)],
            send_sem=g_send.at[way, s, c], recv_sem=g_recv.at[s, c],
            device_id={"rows": to}, device_id_type=MESH,
        )

    def each_shard(do, arrive):
        @pl.loop(0, PARTS)
        def _(c):
            @pl.when(above)
            def _():
                do(g_copy(0, me, c))

            @pl.when(below)
            def _():
                do(g_copy(1, me, c))

            do(g_copy(2, me, c))

        def crossed(h):
            @pl.when(z >= h)
            def _():
                s = beside - 2 * h
                arrive(s, 0)

                @pl.when(above)
                def _():
                    do(g_copy(0, s, 0))

                if h == 0:
                    @pl.when(below)
                    def _():
                        do(g_copy(1, s, 0))

            if h > 0:
                @pl.when(z + h < nz)
                def _():
                    s = beside + 2 * h
                    arrive(s, 0)

                    @pl.when(below)
                    def _():
                        do(g_copy(1, s, 0))

        crossed(0)
        for h in range(1, nz):
            @pl.loop(0, PARTS)
            def _(c):
                @pl.when(z >= h)
                def _():
                    s = me - 2 * h
                    arrive(s, c)

                    @pl.when(above)
                    def _():
                        do(g_copy(0, s, c))

                    @pl.when(c > 0)
                    def _():
                        do(g_copy(2, s, c))

                @pl.when(z + h < nz)
                def _():
                    s = me + 2 * h
                    arrive(s, c)

                    @pl.when(below)
                    def _():
                        do(g_copy(1, s, c))

                    @pl.when(c > 0)
                    def _():
                        do(g_copy(2, s, c))

            crossed(h)

    t_copy.wait()
    each_shard(lambda copy: copy.start(), lambda s, c: g_copy(2, s, c).wait_recv())
    for j in range(nz):
        @pl.loop(1, PARTS)
        def _(c):
            g_copy(2, 2 * j + 1 - y, c).wait_recv()

    def dist_copy(b):
        return pltpu.make_async_remote_copy(
            src_ref=sent.at[b], dst_ref=got.at[b], send_sem=d_send.at[b],
            recv_sem=d_recv.at[b], device_id=partner, device_id_type=MESH,
        )

    def resp_copy(b, part):
        return pltpu.make_async_remote_copy(
            src_ref=resp.at[b, part], dst_ref=resp.at[b, part], send_sem=r_send.at[b],
            recv_sem=r_recv.at[b], device_id=partner, device_id_type=MESH,
        )

    nt = (((1,), (1,)), ((), ()))

    def sweep(index_of, first):
        acc[...] = jnp.zeros_like(acc)
        macc[...] = jnp.zeros_like(macc)

        def body(dist, soft, summed):
            if dist is not None:
                if first:
                    x_copy(dist).wait()
                c = table[index_of(dist)]
                far = x[pl.ds(pl.multiple_of(dist * rows + other * half, half), half), :]
                mine = x[pl.ds(pl.multiple_of(dist * rows + core * half, half), half), :]
            if soft is not None:
                dist_copy(soft).wait()
                logit = (own[soft] + got[soft]) * scale
            if summed is not None:
                resp_copy(summed, core).wait_send()
                resp_copy(summed, other).wait_recv()
                r = jnp.concatenate([resp[summed, 0], resp[summed, 1]], axis=1)
                points = x[pl.ds(pl.multiple_of(summed * rows, rows), rows), :]
                before = slot_ref[jnp.maximum(summed - 1, 0)]
                keep = jnp.where(
                    jnp.logical_and(summed > 0, slot_ref[summed] == before), 1.0, 0.0
                )
            if dist is not None:
                cf = c.astype(F32)
                square = jnp.sum(cf * cf, axis=1, keepdims=True)
                away = 2.0 * lax.dot_general(c, far, nt, preferred_element_type=F32) - square
                sent[dist] = away
                here = 2.0 * lax.dot_general(c, mine, nt, preferred_element_type=F32) - square
                own[dist] = here
            if soft is not None:
                e = jnp.exp2(logit - jnp.max(logit, axis=0, keepdims=True))
                place = lax.broadcasted_iota(jnp.int32, (1, half), 1) + core * half
                used = jnp.where(place < size_ref[soft], 1.0, 0.0)
                resp[soft, core] = (e * (used / jnp.sum(e, axis=0, keepdims=True))).astype(BF)
            if summed is not None:
                total = acc[...] * keep + jnp.dot(r, points, preferred_element_type=F32)
                acc[...] = total
                seg[summed, :, :width] = total.astype(BF)
                tally = macc[...] * keep + jnp.sum(r.astype(F32), axis=1, keepdims=True)
                macc[...] = tally
                lane = lax.broadcasted_iota(jnp.int32, (kids, EXTRA), 1)
                number = slot_ref[summed].astype(F32)
                seg[summed, :, width:] = jnp.where(lane < EXTRA // 2, tally, number).astype(BF)
            if dist is not None:
                dist_copy(dist).start()
            if soft is not None:
                resp_copy(soft, core).start()

        marks = sorted({0, LAG1, LAG2, nb, nb + LAG1, nb + LAG2})
        for lo, hi in zip(marks[:-1], marks[1:]):
            @pl.loop(lo, hi)
            def _(step, lo=lo):
                body(
                    step if lo < nb else None,
                    step - LAG1 if LAG1 <= lo < nb + LAG1 else None,
                    step - LAG2 if LAG2 <= lo else None,
                )

    sweep(lambda b: slot_ref[b], True)

    head, tail = slot_ref[0], slot_ref[nb - 1]
    msg[0] = seg[last_ref[head]]
    msg[1] = seg[nb - 1]

    def near_copy(i, off, c):
        which = 0 if off < 0 else 1
        there = offsets.index(-off)
        return pltpu.make_async_remote_copy(
            src_ref=msg.at[which, part(c)], dst_ref=near.at[there, part(c)],
            send_sem=n_send.at[i, c], recv_sem=n_recv.at[there, c],
            device_id={"rows": me + off}, device_id_type=MESH,
        )

    def arrival(i, c):
        return pltpu.make_async_remote_copy(
            src_ref=msg.at[0, part(c)], dst_ref=near.at[i, part(c)], send_sem=n_send.at[i, c],
            recv_sem=n_recv.at[i, c], device_id={"rows": me}, device_id_type=MESH,
        )

    @pl.loop(0, PARTS)
    def _(c):
        for i, off in enumerate(offsets):
            @pl.when(jnp.logical_and(me + off >= 0, me + off < n))
            def _():
                near_copy(i, off, c).start()

    each_shard(lambda copy: copy.wait_send(), lambda s, c: None)
    table[nslot] = table[head]
    table[nslot + 1] = table[tail]

    def pieces(body):
        @pl.loop(0, kids // CHUNK)
        def _(c):
            body(pl.ds(pl.multiple_of(c * CHUNK, CHUNK), CHUNK))

    @pl.loop(0, nslot)
    def _(q):
        at = last_ref[q]

        def body(r):
            t = seg[at, r, :].astype(F32)
            new = (t[:, :width] + table[q, r, :].astype(F32)) / (t[:, width:width + 1] + 1.0)
            table[q, r, :] = new.astype(BF)

        pieces(body)

    ID = width + EXTRA // 2

    @pl.loop(0, PARTS)
    def _(c):
        for i, off in enumerate(offsets):
            @pl.when(jnp.logical_and(me + off >= 0, me + off < n))
            def _():
                near_copy(i, off, c).wait_send()
                arrival(i, c).wait_recv()

        for which, number in ((0, head), (1, tail)):
            @pl.loop(0, kids // PARTS // 16)
            def _(k):
                r = pl.ds(pl.multiple_of(c * (kids // PARTS) + k * 16, 16), 16)
                t = msg[which, r, :].astype(F32)
                total = t[:, :width] + table[nslot + which, r, :].astype(F32)
                mass = t[:, width:width + 1] + 1.0
                for i in range(len(offsets)):
                    m = near[i, r, :].astype(F32)
                    flag = jnp.where(m[:, ID:ID + 1] == number.astype(F32), 1.0, 0.0)
                    total = total + m[:, :width] * flag
                    mass = mass + m[:, width:width + 1] * flag
                table[nslot + which, r, :] = (total / mass).astype(BF)

    def second(q):
        return jnp.where(q == head, nslot, jnp.where(q == tail, nslot + 1, q))

    sweep(lambda b: second(slot_ref[b]), False)

    def mass_copy(to, source):
        return pltpu.make_async_remote_copy(
            src_ref=mass_out.at[to], dst_ref=mass_in.at[source], send_sem=m_send.at[to],
            recv_sem=m_recv.at[source], device_id={"rows": to}, device_id_type=MESH,
        )

    def make_partial(q):
        at, where = last_ref[q], second(q)
        present = jnp.where(slot_ref[at] == q, 1.0, 0.0)
        is_head = jnp.where(q == head, 1.0, 0.0)

        def body(r):
            t = seg[at, r, :width].astype(F32) * present
            ident = near[0, r, :].astype(F32)[:, ID:ID + 1]
            begun = jnp.where(ident == head.astype(F32), 1.0, 0.0) * is_head
            fold = present * (1.0 - begun)
            table[q, r, :] = (t + fold * table[where, r, :].astype(F32)).astype(BF)

        pieces(body)
        tile = jnp.transpose(seg[at, :, width:].astype(F32)) * present
        mass_out[q] = tile[:mass_out.shape[1], :].astype(BF)

    def y_copy(j, c):
        return pltpu.make_async_remote_copy(
            src_ref=table.at[2 * j + 1 - y, part(c)], dst_ref=ybuf.at[j, part(c)],
            send_sem=y_send.at[j, c], recv_sem=y_recv.at[j, c],
            device_id={"rows": beside}, device_id_type=MESH,
        )

    def z_copy(j, c, to, place):
        return pltpu.make_async_remote_copy(
            src_ref=table.at[2 * j + y, part(c)], dst_ref=zbuf.at[place, part(c)],
            send_sem=z_send.at[j, c], recv_sem=z_recv.at[place, c],
            device_id={"rows": to}, device_id_type=MESH,
        )

    def far_first(body):
        for t in range(nz - 1, 0, -1):
            @pl.when(z + t < nz)
            def _():
                body(t, 1)

            @pl.when(z >= t)
            def _():
                body(t, -1)

        body(0, 0)

    def send_beside(t, sign):
        j = z + sign * t
        make_partial(2 * j + 1 - y)

        @pl.loop(0, PARTS)
        def _(c):
            y_copy(j, c).start()

    far_first(send_beside)
    far_first(lambda t, sign: make_partial(2 * (z + sign * t) + y))
    for off in range(1, n):
        mass_copy(lax.rem(me + off, n), me).start()
    mass_in[me] = mass_out[me]

    def pass_on(t, sign):
        j = z + sign * t
        q = 2 * j + y

        @pl.loop(0, PARTS)
        def _(c):
            r = part(c)
            y_copy(j, c).wait_recv()
            if t > 0:
                table[q, r, :] = (table[q, r, :].astype(F32) + ybuf[j, r, :].astype(F32)).astype(BF)

                @pl.when(below if sign > 0 else above)
                def _():
                    z_copy(j, c, me, j).wait_recv()
                    table[q, r, :] = (
                        table[q, r, :].astype(F32) + zbuf[j, r, :].astype(F32)
                    ).astype(BF)

                if t == 1 and sign < 0:
                    z_copy(j, c, me - 2, nz).start()
                else:
                    z_copy(j, c, me + 2 * sign, j).start()
            else:
                acc[r, :] = table[me, r, :].astype(F32) + ybuf[z, r, :].astype(F32)

    far_first(pass_on)
    for off in range(1, n):
        mass_copy(me, lax.rem(me + off, n)).wait_recv()
    mass = mass_in[0].astype(F32)
    for s in range(1, n):
        mass = mass + mass_in[s].astype(F32)
    mass_ref[...] = mass[:1, :]
    column = jnp.transpose(jnp.broadcast_to(mass[:1, :], (EXTRA, kids)))
    macc[...] = column + 1.0

    @pl.loop(0, PARTS)
    def _(c):
        r = part(c)

        @pl.when(below)
        def _():
            z_copy(z, c, me, z).wait_recv()
            acc[r, :] = acc[r, :] + zbuf[z, r, :].astype(F32)

        @pl.when(above)
        def _():
            z_copy(z, c, me, nz).wait_recv()
            acc[r, :] = acc[r, :] + zbuf[nz, r, :].astype(F32)

        out_ref[0, r, :] = (acc[r, :] / macc[r, :1]).astype(BF)

    def sent_all(t, sign):
        j = z + sign * t

        @pl.loop(0, PARTS)
        def _(c):
            y_copy(j, c).wait_send()
            if t > 0:
                z_copy(j, c, me + 2 * sign, j).wait_send()

    far_first(sent_all)
    for off in range(1, n):
        mass_copy(lax.rem(me + off, n), me).wait_send()


def on_device(embeddings, centroids, block_parent, block_size, owner_slot):
    nb = block_parent.shape[0]
    rows_all, width = embeddings.shape
    kids = centroids.shape[1]
    nslot = owner_slot.shape[0]
    n = lax.axis_size("rows")
    reach = max(2, -(-n // 4))
    half = rows_all // nb // 2
    slot_range = jnp.arange(nslot, dtype=jnp.int32)
    block_slot = jnp.sum(
        jnp.where(block_parent[:, None] == slot_range[None, :], owner_slot[None, :], 0), axis=1
    )
    place = jnp.arange(nb, dtype=jnp.int32)
    last = jnp.max(jnp.where(block_slot[:, None] == slot_range[None, :], place[:, None], 0), axis=0)
    smem = pl.BlockSpec(memory_space=pltpu.SMEM)
    anywhere = pl.BlockSpec(memory_space=pl.ANY)
    dma = pltpu.SemaphoreType.DMA
    vmem = pl.BlockSpec(memory_space=pltpu.VMEM)
    return pl.pallas_call(
        functools.partial(kernel, n, nslot, nb, reach, width * lax.axis_size("inner")),
        out_shape=(
            jax.ShapeDtypeStruct((1, kids, width), BF),
            jax.ShapeDtypeStruct((1, kids), F32),
        ),
        in_specs=[smem, smem, smem, anywhere, anywhere],
        out_specs=(vmem, vmem),
        scratch_shapes=[
            pltpu.VMEM((rows_all, width), BF),
            pltpu.VMEM((nslot + 2, kids, width), BF),
            pltpu.VMEM((nb, kids, half), F32),
            pltpu.VMEM((nb, kids, half), F32),
            pltpu.VMEM((nb, kids, half), F32),
            pltpu.VMEM((nb, 2, kids, half), BF),
            pltpu.VMEM((kids, width), F32),
            pltpu.VMEM((kids, EXTRA), F32),
            pltpu.VMEM((nb, kids, width + EXTRA), BF),
            pltpu.VMEM((2, kids, width + EXTRA), BF),
            pltpu.VMEM((2 * reach, kids, width + EXTRA), BF),
            pltpu.VMEM((n // 2, kids, width), BF),
            pltpu.VMEM((n // 2 + 1, kids, width), BF),
            pltpu.VMEM((n, 16, kids), BF),
            pltpu.VMEM((n, 16, kids), BF),
            dma((nb,)),
            dma,
            dma((nb,)),
            dma((nb,)),
            dma((nb,)),
            dma((nb,)),
            dma((2 * reach, PARTS)),
            dma((2 * reach, PARTS)),
            dma((3, n, PARTS)),
            dma((n, PARTS)),
            dma((n // 2, PARTS)),
            dma((n // 2, PARTS)),
            dma((n // 2, PARTS)),
            dma((n // 2 + 1, PARTS)),
            dma((n,)),
            dma((n,)),
        ],
        compiler_params=pltpu.CompilerParams(
            collective_id=0, has_side_effects=True, vmem_limit_bytes=60 * 1024 * 1024
        ),
        cost_estimate=pl.CostEstimate(
            flops=8 * rows_all * kids * width, bytes_accessed=embeddings.size * 2,
            transcendentals=2 * rows_all * kids // 2,
        ),
    )(block_slot, block_size, last, embeddings, centroids)


def solution(mesh):
    placed = (
        P(("groups", "rows"), "inner"),
        P(("groups", "rows"), None, "inner"),
        P(("groups", "rows")),
        P(("groups", "rows")),
        P("groups"),
    )
    return jax.shard_map(
        on_device,
        mesh=mesh,
        in_specs=placed,
        out_specs=(P(("groups", "rows"), None, "inner"), P(("groups", "rows"), None)),
        check_vma=False,
    )
```
